32 devices in a mesh: dp: 2 (over core), expert: 4 (over y, x), shard: 4 (over z).
Axes of the slice: x: 2, y: 2, z: 4, core: 2. Of those that a mesh axis runs over, the one named last changes fastest.
Arguments:
- tokens: bfloat16 [256, 4096], P('dp', 'shard'), may hold values from -6 to 6
- cotangent: bfloat16 [256, 4096], P('dp', 'shard'), may hold values from -6 to 6
- routes: int32 [256, 2], P('dp'), may hold values from 0 to 3, all different within a row; in each aligned block of 128 rows (0 to 127, 128 to 255, ...) at most 96 rows name the same one
- gate_prob: float32 [256, 2], P('dp'), may hold values from 0.2 to 1
- w_gate: bfloat16 [4, 4096, 8192], P('expert', 'shard', 'dp'), may hold values from -0.09375 to 0.09375
- w_up: bfloat16 [4, 4096, 8192], P('expert', 'shard', 'dp'), may hold values from -0.09375 to 0.09375
- w_down: bfloat16 [4, 8192, 4096], P('expert', 'dp', 'shard'), may hold values from -0.0625 to 0.0625
Outputs:
- mixed: bfloat16 [256, 4096], P('dp', 'shard')
- grad_tokens: bfloat16 [256, 4096], P('dp', 'shard')
- grad_gate: float32 [4, 4096, 8192], P('expert', 'shard', 'dp')
- grad_up: float32 [4, 4096, 8192], P('expert', 'shard', 'dp')
- grad_down: float32 [4, 8192, 4096], P('expert', 'dp', 'shard')
The draws below stay inside these ranges and needn't reach their ends.
Inputs may be any that keep to these rules, and one draw needn't show every extreme that they name: The two routes of a row differ. In each aligned block of 128 rows no expert is named by more than 96 rows.
All inputs are finite; a program needn't handle non-finite values.
Results may differ from the reference program's by a relative error of at most 0.02.
Values may be sent and summed in bfloat16 or wider, within the bound.
A program may use at most 128 MiB of HBM per device.

```python
import math
import jax
import jax.numpy as jnp
import numpy as np
from jax import lax

D = 4096
FF = 8192
TOK_DEV = 128
EXPERTS = 4
CAP = 96
TOKENS = 256
N_DP = 2


def block_scale(key, shape, shards, low, largest):
    level, own = 1.0, jax.random.fold_in(key, 6)
    for axis_at, shards_of in shards:
        draws = jnp.exp(jax.random.uniform(jax.random.fold_in(own, axis_at), (shards_of,), jnp.float32, low / len(shards), largest / len(shards)))
        level = level * jnp.repeat(draws, shape[axis_at] // shards_of).reshape([-1 if axis == axis_at else 1 for axis in range(len(shape))])
    return level


def assign_block(stream_key, own, number, rows, count, top, limit, skew):
    order = jax.random.permutation(stream_key, count)
    packed, common = portions_of(count, rows * top, limit, skew, True), portions_of(count, rows * top, limit, skew, False)
    places = jnp.arange(count)

    def named(tallies, turn):
        used = int((tallies > 0).sum())
        fixed = max(1, used // 4)
        passed = fixed + (places - fixed + turn * (used - fixed)) % max(1, count - fixed)
        return jnp.zeros((count,), jnp.int32).at[order[jnp.where(places < fixed, places, passed)]].set(jnp.asarray(tallies, jnp.int32))

    tallies = jnp.where(number % 4 == 0, named(packed, number // 4), named(common, number - number // 4 - 1))
    mixed = jax.random.permutation(jax.random.fold_in(own, 3), count)
    giver, sink = mixed[0:count // 2 * 2:2], mixed[1:count // 2 * 2:2]
    margin = jnp.minimum(tallies[giver] - 1, limit - tallies[sink]) // 2
    margin = jnp.where((giver == order[0]) | (sink == order[0]) | (tallies[sink] == 0), 0, jnp.maximum(margin, 0))
    passed = jax.random.randint(jax.random.fold_in(own, 4), (count // 2,), 0, 1 << 20) % (margin + 1)
    tallies = tallies.at[giver].add(-passed).at[sink].add(passed)
    members = jnp.searchsorted(jnp.cumsum(tallies), jnp.arange(rows * top), side="right").astype(jnp.int32)
    grid = members.reshape(top, rows).T
    grid = grid[jax.random.permutation(jax.random.fold_in(own, 1), rows)]
    turn = jax.random.randint(jax.random.fold_in(own, 2), (rows, 1), 0, top)
    return jnp.take_along_axis(grid, (jnp.arange(top)[None, :] + turn) % top, axis=1)


def portions_of(number_of, total, limit, skew, full):
    weights = [(1 << 20) // math.isqrt(grade ** skew) + 1 for grade in range(1, number_of + 1)]
    largest = limit if full else min(limit, max(-(-total // number_of), total * weights[0] // sum(weights)))
    least = 1 if total - largest >= number_of - 1 else 0
    given, rest = [largest] + [least] * (number_of - 1), total - largest - least * (number_of - 1)
    while rest > 0:
        free = [i for i in range(1, number_of) if given[i] < largest] or [i for i in range(1, number_of) if given[i] < limit]
        whole, remaining = sum([weights[i] for i in free]), rest
        for i in free:
            addition = min(limit - given[i], max(1, remaining * weights[i] // whole), rest)
            given[i] = given[i] + addition
            rest = rest - addition
    return np.array(given)


def centred(rng, shape, spread, limit, cuts=(), held_as=jnp.bfloat16):
    drawn = jax.random.normal(rng, shape, jnp.float32) * spread
    if len(cuts) > 0:
        drawn = block_scale(rng, shape, cuts, -0.22, 0.18) * drawn
    return jnp.clip(drawn, min=-limit, max=limit).astype(held_as)


def setup_inputs(seed: int = 0) -> dict:
    arg_keys = jax.random.split(jax.random.key(seed), 8)
    tokens = centred(arg_keys[0], (TOKENS, D), 1.0, 6.0, ((0, 2), (1, 4)))
    cotangent = centred(arg_keys[1], (TOKENS, D), 1.0, 6.0, ((0, 2), (1, 4)))
    routes_keys = jax.random.split(jax.random.fold_in(arg_keys[2], 1), TOKENS // TOK_DEV)
    routes_turns = jax.random.permutation(jax.random.fold_in(arg_keys[2], 3), TOKENS // TOK_DEV)
    routes = jax.vmap(lambda own, number: assign_block(jax.random.fold_in(arg_keys[2], 2), own, number, TOK_DEV, EXPERTS, 2, CAP, 2))(routes_keys, routes_turns).reshape((TOKENS, 2))
    gate_prob = jnp.clip(jnp.exp(math.log(1.0) - 1.609438 * jax.random.uniform(arg_keys[3], (TOKENS, 2), jnp.float32) ** block_scale(arg_keys[3], (TOKENS, 2), ((0, 2),), -0.2, 0.2)), 0.2, 1.0)
    w_gate = centred(arg_keys[4], (EXPERTS, D, FF), D ** -0.5, 0.09375, ((0, 4), (1, 4), (2, 2)))
    w_up = centred(arg_keys[5], (EXPERTS, D, FF), D ** -0.5, 0.09375, ((0, 4), (1, 4), (2, 2)))
    w_down = centred(arg_keys[6], (EXPERTS, FF, D), FF ** -0.5, 0.0625, ((0, 4), (1, 2), (2, 4)))
    return dict(tokens=tokens, cotangent=cotangent, routes=routes, gate_prob=gate_prob, w_gate=w_gate, w_up=w_up, w_down=w_down)


def silu_parts(values):
    sigma = jax.nn.sigmoid(values)
    return values * sigma, sigma * (1.0 + values * (1.0 - sigma))


def reference(tokens, cotangent, routes, gate_prob, w_gate, w_up, w_down):
    highest = lax.Precision.HIGHEST
    route_blocks = routes.reshape(N_DP, TOK_DEV, 2)
    prob_blocks = gate_prob.reshape(N_DP, TOK_DEV, 2)
    token_blocks = tokens.reshape(N_DP, TOK_DEV, D).astype(jnp.float32)
    cot_blocks = cotangent.reshape(N_DP, TOK_DEV, D).astype(jnp.float32)
    positions = jnp.arange(TOK_DEV)
    below_mask = (positions[:, None] > positions[None, :]).astype(jnp.float32)
    slot_iota = jnp.arange(CAP).astype(jnp.float32)
    out_total = jnp.zeros((N_DP, TOK_DEV, D), jnp.float32)
    grad_total = jnp.zeros((N_DP, TOK_DEV, D), jnp.float32)
    grads_gate = []
    grads_up = []
    grads_down = []
    for expert in range(EXPERTS):
        chosen = route_blocks == expert
        chosen_rows = jnp.any(chosen, axis=2).astype(jnp.float32)
        weight = jnp.sum(jnp.where(chosen, prob_blocks, 0.0), axis=2)
        slot_rank = jnp.einsum("ts,bs->bt", below_mask, chosen_rows, precision=highest)
        dispatch = (slot_rank[:, :, None] == slot_iota[None, None, :]).astype(jnp.float32) * chosen_rows[:, :, None]
        x_slots = jnp.einsum("btc,btd->bcd", dispatch, token_blocks, precision=highest).astype(jnp.bfloat16).reshape(N_DP * CAP, D)
        dz_tok = (weight[:, :, None] * cot_blocks).astype(jnp.bfloat16).astype(jnp.float32)
        dz_slots = jnp.einsum("btc,btd->bcd", dispatch, dz_tok, precision=highest).astype(jnp.bfloat16).reshape(N_DP * CAP, D)
        gate_value = jnp.dot(x_slots, w_gate[expert], preferred_element_type=jnp.float32)
        up_value = jnp.dot(x_slots, w_up[expert], preferred_element_type=jnp.float32)
        active, slope = silu_parts(gate_value)
        hidden = (active * up_value).astype(jnp.bfloat16)
        d_hidden = jnp.dot(dz_slots, w_down[expert].T, preferred_element_type=jnp.float32)
        d_gate = (d_hidden * up_value * slope).astype(jnp.bfloat16)
        d_up = (d_hidden * active).astype(jnp.bfloat16)
        expert_out = jnp.dot(hidden, w_down[expert], preferred_element_type=jnp.float32)
        slot_grad = jnp.dot(d_gate, w_gate[expert].T, preferred_element_type=jnp.float32) + jnp.dot(d_up, w_up[expert].T, preferred_element_type=jnp.float32)
        grads_down.append(jnp.dot(hidden.T, dz_slots, preferred_element_type=jnp.float32))
        grads_gate.append(jnp.dot(x_slots.T, d_gate, preferred_element_type=jnp.float32))
        grads_up.append(jnp.dot(x_slots.T, d_up, preferred_element_type=jnp.float32))
        out_total = out_total + jnp.einsum("btc,bcd->btd", dispatch * weight[:, :, None], expert_out.reshape(N_DP, CAP, D), precision=highest)
        grad_total = grad_total + jnp.einsum("btc,bcd->btd", dispatch, slot_grad.reshape(N_DP, CAP, D), precision=highest)
    mixed = out_total.reshape(TOKENS, D).astype(jnp.bfloat16)
    grad_tokens = grad_total.reshape(TOKENS, D).astype(jnp.bfloat16)
    return (mixed, grad_tokens, jnp.stack(grads_gate), jnp.stack(grads_up), jnp.stack(grads_down))
```

```python
import functools

import jax
import jax.numpy as jnp
from jax import lax
from jax.experimental import pallas as pl
from jax.experimental.pallas import tpu as pltpu
from jax.sharding import PartitionSpec as P

CAP = 96
WIDTH = 128
AHEAD = 2
MESH = pl.DeviceIdType.MESH
F32 = jnp.float32
BF16 = jnp.bfloat16


def dot_nn(left, right):
    return lax.dot_general(left, right, (((1,), (0,)), ((), ())), preferred_element_type=F32)


def dot_nt(left, right):
    return lax.dot_general(left, right, (((1,), (1,)), ((), ())), preferred_element_type=F32)


def dot_tn(left, right):
    return lax.dot_general(left, right, (((0,), (0,)), ((), ())), preferred_element_type=F32)


def exchange_kernel(
    n, n_dp, chunks,
    tok, cot, routes, prob, wg, wu, wd,
    tok_out, act_out, x_out, dz_out,
    wgv, wuv, wdv, part, from_left, from_right, to_right, to_left,
    x_v, dz_v, acc_o, acc_g, stage, landed, disp, wgt,
    w_sem, sr_sem, rr_sem, sl_sem, rl_sem, act_sem, xo_sem,
    xs_sem, xr_sem, os_sem, or_sem,
):
    f = WIDTH
    s = lax.axis_index("shard")
    d = lax.axis_index("dp")
    e = lax.axis_index("expert")
    act = from_left
    n_part = part.shape[0]
    n_stage = to_right.shape[0]
    t = tok.shape[0]

    def w_copies(c):
        cols = pl.ds(pl.multiple_of(c * f, f), f)
        return (
            pltpu.make_async_copy(wg.at[:, cols], wgv.at[c], w_sem.at[0, c]),
            pltpu.make_async_copy(wu.at[:, cols], wuv.at[c], w_sem.at[1, c]),
            pltpu.make_async_copy(wd.at[cols, :], wdv.at[c], w_sem.at[2, c]),
        )

    @pl.loop(0, chunks)
    def _(c):
        for copy in w_copies(c):
            copy.start()

    barrier = pltpu.get_barrier_semaphore()

    @pl.when(s > 0)
    def _():
        pl.semaphore_signal(barrier, inc=1, device_id={"shard": s - 1}, device_id_type=MESH)

    @pl.when(s < n - 1)
    def _():
        pl.semaphore_signal(barrier, inc=1, device_id={"shard": s + 1}, device_id_type=MESH)

    for k in range(1, n_dp):
        pl.semaphore_signal(
            barrier, inc=1, device_id={"dp": lax.rem(d + k, n_dp)}, device_id_type=MESH
        )

    chosen = routes[...] == e
    picked = jnp.max(chosen.astype(F32), axis=1, keepdims=True)
    weight = jnp.sum(jnp.where(chosen, prob[...], 0.0), axis=1, keepdims=True)
    rows_i = lax.broadcasted_iota(jnp.int32, (t, t), 0)
    cols_i = lax.broadcasted_iota(jnp.int32, (t, t), 1)
    below = (rows_i > cols_i).astype(F32).astype(BF16)
    rank = dot_nn(below, jnp.broadcast_to(picked, (t, t)).astype(BF16))[:, :CAP]
    slot = lax.broadcasted_iota(jnp.int32, (t, CAP), 1).astype(F32)
    dispatch = jnp.where(rank == slot, jnp.broadcast_to(picked, (t, CAP)), 0.0).astype(BF16)
    disp[...] = dispatch
    wgt[...] = jnp.broadcast_to(weight, wgt.shape)
    mine = pl.ds(pl.multiple_of(d * CAP, CAP), CAP)
    x_v[mine, :] = dot_tn(dispatch, tok[...]).astype(BF16)
    dz_tok = (weight * cot[...].astype(F32)).astype(BF16)
    dz_v[mine, :] = dot_tn(dispatch, dz_tok).astype(BF16)

    pl.semaphore_wait(barrier, (s > 0).astype(jnp.int32) + (s < n - 1).astype(jnp.int32) + (n_dp - 1))

    def slot_copy(ref, k, row, sem_row, to):
        rows = pl.ds(pl.multiple_of(row * CAP, CAP), CAP)
        return pltpu.make_async_remote_copy(
            src_ref=ref.at[rows], dst_ref=ref.at[rows],
            send_sem=xs_sem.at[k, to], recv_sem=xr_sem.at[k, sem_row],
            device_id={"dp": to}, device_id_type=MESH,
        )

    for j in range(1, n_dp):
        to = lax.rem(d + j, n_dp)
        slot_copy(x_v, 0, d, d, to).start()
        slot_copy(dz_v, 1, d, d, to).start()
    acc_o[...] = jnp.zeros_like(acc_o)
    acc_g[...] = jnp.zeros_like(acc_g)
    for j in range(1, n_dp):
        other = lax.rem(d + j, n_dp)
        slot_copy(x_v, 0, other, other, other).wait_recv()
        slot_copy(dz_v, 1, other, other, other).wait_recv()
    for j in range(1, n_dp):
        to = lax.rem(d + j, n_dp)
        slot_copy(x_v, 0, d, d, to).wait_send()
        slot_copy(dz_v, 1, d, d, to).wait_send()
    x_store = pltpu.make_async_copy(x_v, x_out, xo_sem.at[0])
    dz_store = pltpu.make_async_copy(dz_v, dz_out, xo_sem.at[1])
    x_store.start()
    dz_store.start()

    def right_copy(c):
        here = lax.rem(c, n_stage)
        return pltpu.make_async_remote_copy(
            src_ref=to_right.at[here], dst_ref=from_left.at[c],
            send_sem=sr_sem.at[here], recv_sem=rr_sem.at[c],
            device_id={"shard": lax.min(s + 1, n - 1)}, device_id_type=MESH,
        )

    def left_copy(c):
        here = lax.rem(c, n_stage)
        return pltpu.make_async_remote_copy(
            src_ref=to_left.at[here], dst_ref=from_right.at[c],
            send_sem=sl_sem.at[here], recv_sem=rl_sem.at[c],
            device_id={"shard": lax.max(s - 1, 0)}, device_id_type=MESH,
        )

    def send(copy_of, buffer, c, value):
        @pl.when(c >= n_stage)
        def _():
            copy_of(c - n_stage).wait_send()

        buffer[lax.rem(c, n_stage)] = value().astype(BF16)
        copy_of(c).start()

    @pl.loop(0, chunks + AHEAD + n - 1)
    def _(i):
        @pl.when(i < chunks)
        def _():
            for copy in w_copies(i):
                copy.wait()
            p = lax.rem(i, n_part)
            part[p, :, 0:f] = dot_nn(x_v[...], wgv[i])
            part[p, :, f:2 * f] = dot_nn(x_v[...], wuv[i])
            part[p, :, 2 * f:3 * f] = dot_nt(dz_v[...], wdv[i])

            @pl.when((s == 0) & (n > 1))
            def _():
                send(right_copy, to_right, i, lambda: part[p])

            @pl.when((s == n - 1) & (n > 1))
            def _():
                send(left_copy, to_left, i, lambda: part[p])

        r = i - AHEAD - s

        @pl.when((s > 0) & (r >= 0) & (r < chunks))
        def _():
            right_copy(r).wait_recv()

            @pl.when(s < n - 1)
            def _():
                send(right_copy, to_right, r, lambda: part[lax.rem(r, n_part)] + from_left[r].astype(F32))

        q = i - AHEAD - (n - 1 - s)

        @pl.when((s < n - 1) & (q >= 0) & (q < chunks))
        def _():
            left_copy(q).wait_recv()

            @pl.when(s > 0)
            def _():
                send(left_copy, to_left, q, lambda: part[lax.rem(q, n_part)] + from_right[q].astype(F32))

        c = i - AHEAD - lax.max(s, n - 1 - s)

        @pl.when((c >= 0) & (c < chunks))
        def _():
            p = lax.rem(c, n_part)

            @pl.when(s > 0)
            def _():
                part[p] += from_left[c].astype(F32)

            @pl.when(s < n - 1)
            def _():
                part[p] += from_right[c].astype(F32)

            gate = part[p, :, 0:f]
            up = part[p, :, f:2 * f]
            d_hidden = part[p, :, 2 * f:3 * f]
            sigma = jax.nn.sigmoid(gate)
            active = gate * sigma
            slope = sigma * (1.0 + gate * (1.0 - sigma))
            hidden = (active * up).astype(BF16)
            d_gate = (d_hidden * up * slope).astype(BF16)
            d_up = (d_hidden * active).astype(BF16)
            act[c, :, 0:f] = hidden
            act[c, :, f:2 * f] = d_gate
            act[c, :, 2 * f:3 * f] = d_up
            pltpu.make_async_copy(act.at[c], act_out.at[c], act_sem.at[c]).start()
            acc_o[...] += dot_nn(hidden, wdv[c])
            acc_g[...] += dot_nt(d_gate, wgv[c]) + dot_nt(d_up, wuv[c])

    stage[0] = acc_o[...].astype(BF16)
    stage[1] = acc_g[...].astype(BF16)

    def sum_copy(k, to, sender):
        return pltpu.make_async_remote_copy(
            src_ref=stage.at[k, pl.ds(pl.multiple_of(to * CAP, CAP), CAP)],
            dst_ref=landed.at[k, pl.ds(pl.multiple_of(sender * CAP, CAP), CAP)],
            send_sem=os_sem.at[k, to], recv_sem=or_sem.at[k, sender],
            device_id={"dp": to}, device_id_type=MESH,
        )

    for k in range(2):
        for j in range(1, n_dp):
            sum_copy(k, lax.rem(d + j, n_dp), d).start()
    for k in range(2):
        own = (acc_o, acc_g)[k][mine, :]
        for j in range(1, n_dp):
            other = lax.rem(d + j, n_dp)
            sum_copy(k, other, other).wait_recv()
            own = own + landed[k, pl.ds(pl.multiple_of(other * CAP, CAP), CAP), :].astype(F32)
        rows = dot_nn(disp[...], own.astype(BF16))
        if k == 0:
            rows = rows * wgt[:, 0:1]
        tok_out[k] = rows.astype(BF16)

    for k in range(2):
        for j in range(1, n_dp):
            sum_copy(k, lax.rem(d + j, n_dp), d).wait_send()
    x_store.wait()
    dz_store.wait()

    @pl.loop(0, chunks)
    def _(c):
        pltpu.make_async_copy(act.at[c], act_out.at[c], act_sem.at[c]).wait()

    @pl.loop(max(chunks - n_stage, 0), chunks)
    def _(c):
        @pl.when(s < n - 1)
        def _():
            right_copy(c).wait_send()

        @pl.when(s > 0)
        def _():
            left_copy(c).wait_send()


def grads_kernel(act, x, dz, gate_out, up_out, down_out, x_t):
    f = WIDTH

    @pl.when(pl.program_id(0) == 0)
    def _():
        x_t[...] = x[...].T

    for c in range(act.shape[0]):
        cols = slice(c * f, (c + 1) * f)
        gate_out[:, cols] = dot_nn(x_t[...], act[c, :, f:2 * f])
        up_out[:, cols] = dot_nn(x_t[...], act[c, :, 2 * f:3 * f])
        down_out[cols, :] = dot_tn(act[c, :, 0:f], dz[...])


def per_device(n, n_dp, tokens, cotangent, routes, gate_prob, w_gate, w_up, w_down):
    t, dl = tokens.shape
    ffl = w_gate.shape[2]
    f = WIDTH
    chunks = ffl // f
    rows = n_dp * CAP
    n_part = min(n + AHEAD, chunks)
    n_stage = max(1, min(4, chunks // 2))
    vmem = pl.BlockSpec(memory_space=pltpu.VMEM)
    hbm = pl.BlockSpec(memory_space=pl.ANY)
    tok_part, act, x_all, dz_all = pl.pallas_call(
        functools.partial(exchange_kernel, n, n_dp, chunks),
        out_shape=(
            jax.ShapeDtypeStruct((2, t, dl), BF16),
            jax.ShapeDtypeStruct((chunks, rows, 3 * f), BF16),
            jax.ShapeDtypeStruct((rows, dl), BF16),
            jax.ShapeDtypeStruct((rows, dl), BF16),
        ),
        in_specs=[vmem] * 4 + [hbm] * 3,
        out_specs=(vmem, hbm, hbm, hbm),
        scratch_shapes=[
            pltpu.VMEM((chunks, dl, f), BF16),
            pltpu.VMEM((chunks, dl, f), BF16),
            pltpu.VMEM((chunks, f, dl), BF16),
            pltpu.VMEM((n_part, rows, 3 * f), F32),
            pltpu.VMEM((chunks, rows, 3 * f), BF16),
            pltpu.VMEM((chunks, rows, 3 * f), BF16),
            pltpu.VMEM((n_stage, rows, 3 * f), BF16),
            pltpu.VMEM((n_stage, rows, 3 * f), BF16),
            pltpu.VMEM((rows, dl), BF16),
            pltpu.VMEM((rows, dl), BF16),
            pltpu.VMEM((rows, dl), F32),
            pltpu.VMEM((rows, dl), F32),
            pltpu.VMEM((2, rows, dl), BF16),
            pltpu.VMEM((2, rows, dl), BF16),
            pltpu.VMEM((t, CAP), BF16),
            pltpu.VMEM((t, 128), F32),
            pltpu.SemaphoreType.DMA((3, chunks)),
            pltpu.SemaphoreType.DMA((n_stage,)),
            pltpu.SemaphoreType.DMA((chunks,)),
            pltpu.SemaphoreType.DMA((n_stage,)),
            pltpu.SemaphoreType.DMA((chunks,)),
            pltpu.SemaphoreType.DMA((chunks,)),
            pltpu.SemaphoreType.DMA((2,)),
            pltpu.SemaphoreType.DMA((2, n_dp)),
            pltpu.SemaphoreType.DMA((2, n_dp)),
            pltpu.SemaphoreType.DMA((2, n_dp)),
            pltpu.SemaphoreType.DMA((2, n_dp)),
        ],
        compiler_params=pltpu.CompilerParams(
            collective_id=0, has_side_effects=True, vmem_limit_bytes=63 * 1024 * 1024
        ),
        cost_estimate=pl.CostEstimate(
            flops=12 * rows * dl * ffl, bytes_accessed=6 * dl * ffl, transcendentals=rows * ffl
        ),
    )(tokens, cotangent, routes, gate_prob, w_gate[0], w_up[0], w_down[0])
    total = lax.psum(tok_part, "expert")
    group = next(g for g in (4, 2, 1) if chunks % g == 0)
    grad_gate, grad_up, grad_down = pl.pallas_call(
        grads_kernel,
        grid=(chunks // group,),
        out_shape=(
            jax.ShapeDtypeStruct((dl, ffl), F32),
            jax.ShapeDtypeStruct((dl, ffl), F32),
            jax.ShapeDtypeStruct((ffl, dl), F32),
        ),
        in_specs=[
            pl.BlockSpec((group, rows, 3 * f), lambda j: (j, 0, 0)),
            pl.BlockSpec((rows, dl), lambda j: (0, 0)),
            pl.BlockSpec((rows, dl), lambda j: (0, 0)),
        ],
        out_specs=(
            pl.BlockSpec((dl, group * f), lambda j: (0, j)),
            pl.BlockSpec((dl, group * f), lambda j: (0, j)),
            pl.BlockSpec((group * f, dl), lambda j: (j, 0)),
        ),
        scratch_shapes=[pltpu.VMEM((dl, rows), BF16)],
        compiler_params=pltpu.CompilerParams(vmem_limit_bytes=48 * 1024 * 1024),
        cost_estimate=pl.CostEstimate(
            flops=6 * rows * dl * ffl, bytes_accessed=12 * dl * ffl, transcendentals=0
        ),
    )(act, x_all, dz_all)
    return (total[0], total[1], grad_gate[None], grad_up[None], grad_down[None])


def solution(mesh):
    return jax.shard_map(
        functools.partial(per_device, mesh.shape["shard"], mesh.shape["dp"]),
        mesh=mesh,
        in_specs=(
            P("dp", "shard"),
            P("dp", "shard"),
            P("dp", None),
            P("dp", None),
            P("expert", "shard", "dp"),
            P("expert", "shard", "dp"),
            P("expert", "dp", "shard"),
        ),
        out_specs=(
            P("dp", "shard"),
            P("dp", "shard"),
            P("expert", "shard", "dp"),
            P("expert", "shard", "dp"),
            P("expert", "dp", "shard"),
        ),
        check_vma=False,
    )
```

```python
import functools

import jax
import jax.numpy as jnp
from jax import lax
from jax.experimental import pallas as pl
from jax.experimental.pallas import tpu as pltpu
from jax.sharding import PartitionSpec as P

CAP = 96
WIDTH = 128
HOP = 3
EARLY = 8
MESH = pl.DeviceIdType.MESH
F32 = jnp.float32
BF16 = jnp.bfloat16


def dot_nn(left, right):
    return lax.dot_general(left, right, (((1,), (0,)), ((), ())), preferred_element_type=F32)


def dot_nt(left, right):
    return lax.dot_general(left, right, (((1,), (1,)), ((), ())), preferred_element_type=F32)


def dot_tn(left, right):
    return lax.dot_general(left, right, (((0,), (0,)), ((), ())), preferred_element_type=F32)


def exchange_kernel(
    n, n_dp, chunks,
    tok, cot, routes, prob, wg, wu, wd,
    mix_out, grad_out, act_out, x_out, dz_out,
    wgv, wuv, wdv, part, from_left, from_right, to_right, to_left,
    x_v, dz_v, acc_o, acc_g, stage, landed, disp, wgt,
    w_sem, sr_sem, rr_sem, sl_sem, rl_sem, act_sem, xo_sem,
    xs_sem, xr_sem, os_sem, or_sem,
):
    f = WIDTH
    s = lax.axis_index("shard")
    d = lax.axis_index("dp")
    e = lax.axis_index("expert")
    act = from_left
    n_part = part.shape[0]
    n_stage = to_right.shape[0]
    t = tok.shape[0]

    def w_copies(c):
        cols = pl.ds(pl.multiple_of(c * f, f), f)
        return (
            pltpu.make_async_copy(wg.at[:, cols], wgv.at[c], w_sem.at[0, c]),
            pltpu.make_async_copy(wu.at[:, cols], wuv.at[c], w_sem.at[1, c]),
            pltpu.make_async_copy(wd.at[cols, :], wdv.at[c], w_sem.at[2, c]),
        )

    @pl.loop(0, min(EARLY, chunks))
    def _(c):
        for copy in w_copies(c):
            copy.start()

    barrier = pltpu.get_barrier_semaphore()

    @pl.when(s > 0)
    def _():
        pl.semaphore_signal(barrier, inc=1, device_id={"shard": s - 1}, device_id_type=MESH)

    @pl.when(s < n - 1)
    def _():
        pl.semaphore_signal(barrier, inc=1, device_id={"shard": s + 1}, device_id_type=MESH)

    for k in range(1, n_dp):
        pl.semaphore_signal(
            barrier, inc=1, device_id={"dp": lax.rem(d + k, n_dp)}, device_id_type=MESH
        )

    chosen = routes[...] == e
    picked = jnp.max(chosen.astype(F32), axis=0, keepdims=True)
    weight_row = jnp.sum(jnp.where(chosen, prob[...], 0.0), axis=0, keepdims=True)
    weight = jnp.broadcast_to(weight_row, (t, t)).T[:, 0:1]
    rows_i = lax.broadcasted_iota(jnp.int32, (t, t), 0)
    cols_i = lax.broadcasted_iota(jnp.int32, (t, t), 1)
    above = (rows_i < cols_i).astype(F32).astype(BF16)
    rank = dot_nn(jnp.broadcast_to(picked, (CAP, t)).astype(BF16), above)
    slot = lax.broadcasted_iota(jnp.int32, (CAP, t), 0).astype(F32)
    dispatch = jnp.where(rank == slot, jnp.broadcast_to(picked, (CAP, t)), 0.0).astype(BF16)
    disp[...] = dispatch
    wgt[...] = jnp.broadcast_to(weight, wgt.shape)
    mine = pl.ds(pl.multiple_of(d * CAP, CAP), CAP)
    x_v[mine, :] = dot_nn(dispatch, tok[...]).astype(BF16)
    dz_tok = (weight * cot[...].astype(F32)).astype(BF16)
    dz_v[mine, :] = dot_nn(dispatch, dz_tok).astype(BF16)

    pl.semaphore_wait(barrier, (s > 0).astype(jnp.int32) + (s < n - 1).astype(jnp.int32) + (n_dp - 1))

    def slot_copy(ref, k, row, sem_row, to):
        rows = pl.ds(pl.multiple_of(row * CAP, CAP), CAP)
        return pltpu.make_async_remote_copy(
            src_ref=ref.at[rows], dst_ref=ref.at[rows],
            send_sem=xs_sem.at[k, to], recv_sem=xr_sem.at[k, sem_row],
            device_id={"dp": to}, device_id_type=MESH,
        )

    for j in range(1, n_dp):
        to = lax.rem(d + j, n_dp)
        slot_copy(x_v, 0, d, d, to).start()
        slot_copy(dz_v, 1, d, d, to).start()
    acc_o[...] = jnp.zeros_like(acc_o)
    acc_g[...] = jnp.zeros_like(acc_g)
    for j in range(1, n_dp):
        other = lax.rem(d + j, n_dp)
        slot_copy(x_v, 0, other, other, other).wait_recv()
        slot_copy(dz_v, 1, other, other, other).wait_recv()
    for j in range(1, n_dp):
        to = lax.rem(d + j, n_dp)
        slot_copy(x_v, 0, d, d, to).wait_send()
        slot_copy(dz_v, 1, d, d, to).wait_send()
    x_store = pltpu.make_async_copy(x_v, x_out, xo_sem.at[0])
    dz_store = pltpu.make_async_copy(dz_v, dz_out, xo_sem.at[1])
    x_store.start()
    dz_store.start()

    def right_copy(c):
        here = lax.rem(c, n_stage)
        return pltpu.make_async_remote_copy(
            src_ref=to_right.at[here], dst_ref=from_left.at[c],
            send_sem=sr_sem.at[here], recv_sem=rr_sem.at[c],
            device_id={"shard": lax.min(s + 1, n - 1)}, device_id_type=MESH,
        )

    def left_copy(c):
        here = lax.rem(c, n_stage)
        return pltpu.make_async_remote_copy(
            src_ref=to_left.at[here], dst_ref=from_right.at[c],
            send_sem=sl_sem.at[here], recv_sem=rl_sem.at[c],
            device_id={"shard": lax.max(s - 1, 0)}, device_id_type=MESH,
        )

    def send(copy_of, buffer, c, value):
        @pl.when(c >= n_stage)
        def _():
            copy_of(c - n_stage).wait_send()

        buffer[lax.rem(c, n_stage)] = value().astype(BF16)
        copy_of(c).start()

    @pl.loop(0, chunks + HOP * (n - 1))
    def _(i):
        @pl.when(i < chunks)
        def _():
            for copy in w_copies(i):
                copy.wait()

            @pl.when(i + EARLY < chunks)
            def _():
                for copy in w_copies(i + EARLY):
                    copy.start()

            p = lax.rem(i, n_part)
            part[p, :, 0:f] = dot_nn(x_v[...], wgv[i])
            part[p, :, f:2 * f] = dot_nn(x_v[...], wuv[i])
            part[p, :, 2 * f:3 * f] = dot_nt(dz_v[...], wdv[i])

            @pl.when((s == 0) & (n > 1))
            def _():
                send(right_copy, to_right, i, lambda: part[p])

            @pl.when((s == n - 1) & (n > 1))
            def _():
                send(left_copy, to_left, i, lambda: part[p])

        r = i - HOP * s

        @pl.when((s > 0) & (r >= 0) & (r < chunks))
        def _():
            right_copy(r).wait_recv()

            @pl.when(s < n - 1)
            def _():
                send(right_copy, to_right, r, lambda: part[lax.rem(r, n_part)] + from_left[r].astype(F32))

        q = i - HOP * (n - 1 - s)

        @pl.when((s < n - 1) & (q >= 0) & (q < chunks))
        def _():
            left_copy(q).wait_recv()

            @pl.when(s > 0)
            def _():
                send(left_copy, to_left, q, lambda: part[lax.rem(q, n_part)] + from_right[q].astype(F32))

        c = i - HOP * lax.max(s, n - 1 - s)

        @pl.when((c >= 0) & (c < chunks))
        def _():
            p = lax.rem(c, n_part)

            @pl.when(s > 0)
            def _():
                part[p] += from_left[c].astype(F32)

            @pl.when(s < n - 1)
            def _():
                part[p] += from_right[c].astype(F32)

            gate = part[p, :, 0:f]
            up = part[p, :, f:2 * f]
            d_hidden = part[p, :, 2 * f:3 * f]
            sigma = jax.nn.sigmoid(gate)
            active = gate * sigma
            slope = sigma * (1.0 + gate * (1.0 - sigma))
            hidden = (active * up).astype(BF16)
            d_gate = (d_hidden * up * slope).astype(BF16)
            d_up = (d_hidden * active).astype(BF16)
            act[c, :, 0:f] = hidden
            act[c, :, f:2 * f] = d_gate
            act[c, :, 2 * f:3 * f] = d_up
            pltpu.make_async_copy(act.at[c], act_out.at[c], act_sem.at[c]).start()
            acc_o[...] += dot_nn(hidden, wdv[c])
            acc_g[...] += dot_nt(d_gate, wgv[c]) + dot_nt(d_up, wuv[c])

    stage[0] = acc_o[...].astype(BF16)
    stage[1] = acc_g[...].astype(BF16)

    def sum_copy(k, to, sender):
        return pltpu.make_async_remote_copy(
            src_ref=stage.at[k, pl.ds(pl.multiple_of(to * CAP, CAP), CAP)],
            dst_ref=landed.at[k, pl.ds(pl.multiple_of(sender * CAP, CAP), CAP)],
            send_sem=os_sem.at[k, to], recv_sem=or_sem.at[k, sender],
            device_id={"dp": to}, device_id_type=MESH,
        )

    for k in range(2):
        for j in range(1, n_dp):
            sum_copy(k, lax.rem(d + j, n_dp), d).start()
    for k in range(2):
        own = (acc_o, acc_g)[k][mine, :]
        for j in range(1, n_dp):
            other = lax.rem(d + j, n_dp)
            sum_copy(k, other, other).wait_recv()
            own = own + landed[k, pl.ds(pl.multiple_of(other * CAP, CAP), CAP), :].astype(F32)
        rows = dot_tn(disp[...], own.astype(BF16))
        if k == 0:
            rows = rows * wgt[:, 0:1]
        (mix_out, grad_out)[k][...] = rows.astype(BF16)

    for k in range(2):
        for j in range(1, n_dp):
            sum_copy(k, lax.rem(d + j, n_dp), d).wait_send()
    x_store.wait()
    dz_store.wait()

    @pl.loop(0, chunks)
    def _(c):
        pltpu.make_async_copy(act.at[c], act_out.at[c], act_sem.at[c]).wait()

    @pl.loop(max(chunks - n_stage, 0), chunks)
    def _(c):
        @pl.when(s < n - 1)
        def _():
            right_copy(c).wait_send()

        @pl.when(s > 0)
        def _():
            left_copy(c).wait_send()


def grads_in_kernel(act, x, gate_out, up_out, x_t):
    f = WIDTH

    @pl.when(pl.program_id(0) == 0)
    def _():
        x_t[...] = x[...].T

    for c in range(act.shape[0]):
        cols = slice(c * f, (c + 1) * f)
        gate_out[:, cols] = dot_nn(x_t[...], act[c, :, f:2 * f])
        up_out[:, cols] = dot_nn(x_t[...], act[c, :, 2 * f:3 * f])


def grad_down_kernel(act, dz, down_out):
    f = WIDTH
    for c in range(act.shape[0]):
        down_out[c * f:(c + 1) * f, :] = dot_tn(act[c, :, 0:f], dz[...])


def expert_sum(value, n_expert, bits):
    for bit in bits:
        other = lax.ppermute(value, "expert", [(i, i ^ bit) for i in range(n_expert)])
        value = (value.astype(F32) + other.astype(F32)).astype(BF16)
    return value


def per_device(n, n_dp, n_expert, tokens, cotangent, routes, gate_prob, w_gate, w_up, w_down):
    t, dl = tokens.shape
    ffl = w_gate.shape[2]
    f = WIDTH
    chunks = ffl // f
    rows = n_dp * CAP
    n_part = min(HOP * (n - 1) + 1, chunks)
    n_stage = max(1, min(4, chunks // 2))
    vmem = pl.BlockSpec(memory_space=pltpu.VMEM)
    hbm = pl.BlockSpec(memory_space=pl.ANY)
    mix_part, grad_part, act, x_all, dz_all = pl.pallas_call(
        functools.partial(exchange_kernel, n, n_dp, chunks),
        out_shape=(
            jax.ShapeDtypeStruct((t, dl), BF16),
            jax.ShapeDtypeStruct((t, dl), BF16),
            jax.ShapeDtypeStruct((chunks, rows, 3 * f), BF16),
            jax.ShapeDtypeStruct((rows, dl), BF16),
            jax.ShapeDtypeStruct((rows, dl), BF16),
        ),
        in_specs=[vmem] * 4 + [hbm] * 3,
        out_specs=(vmem, vmem, hbm, hbm, hbm),
        scratch_shapes=[
            pltpu.VMEM((chunks, dl, f), BF16),
            pltpu.VMEM((chunks, dl, f), BF16),
            pltpu.VMEM((chunks, f, dl), BF16),
            pltpu.VMEM((n_part, rows, 3 * f), F32),
            pltpu.VMEM((chunks, rows, 3 * f), BF16),
            pltpu.VMEM((chunks, rows, 3 * f), BF16),
            pltpu.VMEM((n_stage, rows, 3 * f), BF16),
            pltpu.VMEM((n_stage, rows, 3 * f), BF16),
            pltpu.VMEM((rows, dl), BF16),
            pltpu.VMEM((rows, dl), BF16),
            pltpu.VMEM((rows, dl), F32),
            pltpu.VMEM((rows, dl), F32),
            pltpu.VMEM((2, rows, dl), BF16),
            pltpu.VMEM((2, rows, dl), BF16),
            pltpu.VMEM((CAP, t), BF16),
            pltpu.VMEM((t, 128), F32),
            pltpu.SemaphoreType.DMA((3, chunks)),
            pltpu.SemaphoreType.DMA((n_stage,)),
            pltpu.SemaphoreType.DMA((chunks,)),
            pltpu.SemaphoreType.DMA((n_stage,)),
            pltpu.SemaphoreType.DMA((chunks,)),
            pltpu.SemaphoreType.DMA((chunks,)),
            pltpu.SemaphoreType.DMA((2,)),
            pltpu.SemaphoreType.DMA((2, n_dp)),
            pltpu.SemaphoreType.DMA((2, n_dp)),
            pltpu.SemaphoreType.DMA((2, n_dp)),
            pltpu.SemaphoreType.DMA((2, n_dp)),
        ],
        compiler_params=pltpu.CompilerParams(
            collective_id=0, has_side_effects=True, vmem_limit_bytes=63 * 1024 * 1024
        ),
        cost_estimate=pl.CostEstimate(
            flops=12 * rows * dl * ffl, bytes_accessed=6 * dl * ffl, transcendentals=rows * ffl
        ),
    )(tokens, cotangent, routes.T, gate_prob.T, w_gate[0], w_up[0], w_down[0])
    bits = [1 << k for k in range((n_expert - 1).bit_length())]
    mixed = expert_sum(mix_part, n_expert, bits)
    grad_tokens = expert_sum(grad_part, n_expert, bits[::-1])
    group = next(g for g in (4, 2, 1) if chunks % g == 0)
    full = pl.BlockSpec((rows, dl), lambda j: (0, 0))
    act_block = pl.BlockSpec((group, rows, 3 * f), lambda j: (j, 0, 0))
    wide = pl.BlockSpec((dl, group * f), lambda j: (0, j))
    roomy = pltpu.CompilerParams(vmem_limit_bytes=60 * 1024 * 1024)
    grad_gate, grad_up = pl.pallas_call(
        grads_in_kernel,
        grid=(chunks // group,),
        out_shape=(jax.ShapeDtypeStruct((dl, ffl), F32),) * 2,
        in_specs=[act_block, full],
        out_specs=(wide, wide),
        scratch_shapes=[pltpu.VMEM((dl, rows), BF16)],
        compiler_params=roomy,
        cost_estimate=pl.CostEstimate(
            flops=4 * rows * dl * ffl, bytes_accessed=8 * dl * ffl, transcendentals=0
        ),
    )(act, x_all)
    grad_down = pl.pallas_call(
        grad_down_kernel,
        grid=(chunks // group,),
        out_shape=jax.ShapeDtypeStruct((ffl, dl), F32),
        in_specs=[act_block, full],
        out_specs=pl.BlockSpec((group * f, dl), lambda j: (j, 0)),
        compiler_params=roomy,
        cost_estimate=pl.CostEstimate(
            flops=2 * rows * dl * ffl, bytes_accessed=4 * dl * ffl, transcendentals=0
        ),
    )(act, dz_all)
    return (mixed, grad_tokens, grad_gate[None], grad_up[None], grad_down[None])


def solution(mesh):
    return jax.shard_map(
        functools.partial(per_device, mesh.shape["shard"], mesh.shape["dp"], mesh.shape["expert"]),
        mesh=mesh,
        in_specs=(
            P("dp", "shard"),
            P("dp", "shard"),
            P("dp", None),
            P("dp", None),
            P("expert", "shard", "dp"),
            P("expert", "shard", "dp"),
            P("expert", "dp", "shard"),
        ),
        out_specs=(
            P("dp", "shard"),
            P("dp", "shard"),
            P("expert", "shard", "dp"),
            P("expert", "shard", "dp"),
            P("expert", "dp", "shard"),
        ),
        check_vma=False,
    )
```

```python
import functools

import jax
import jax.numpy as jnp
from jax import lax
from jax.experimental import pallas as pl
from jax.experimental.pallas import tpu as pltpu
from jax.sharding import PartitionSpec as P

CAP = 96
WIDTH = 128
HOP = 3
EARLY = 8
HALVES = 2
MESH = pl.DeviceIdType.MESH
F32 = jnp.float32
BF16 = jnp.bfloat16


def dot_nn(left, right):
    return lax.dot_general(left, right, (((1,), (0,)), ((), ())), preferred_element_type=F32)


def dot_nt(left, right):
    return lax.dot_general(left, right, (((1,), (1,)), ((), ())), preferred_element_type=F32)


def dot_tn(left, right):
    return lax.dot_general(left, right, (((0,), (0,)), ((), ())), preferred_element_type=F32)


def exchange_kernel(
    n, n_dp, chunks,
    tok, cot, routes, prob, wg, wu, wd,
    mix_out, grad_out, act_out, x_out, dz_out,
    wguv, wdv, part, from_left, from_right, to_right, to_left,
    x_v, dz_v, acc_o, acc_g, stage, landed, disp, wgt,
    w_sem, sr_sem, rr_sem, sl_sem, rl_sem, act_sem, xo_sem,
    xs_sem, xr_sem, os_sem, or_sem,
):
    f = WIDTH
    s = lax.axis_index("shard")
    d = lax.axis_index("dp")
    e = lax.axis_index("expert")
    act = from_left
    n_part = part.shape[0]
    n_stage = to_right.shape[0]
    t = tok.shape[0]
    half = part.shape[1] // HALVES

    def w_copies(c):
        cols = pl.ds(pl.multiple_of(c * f, f), f)
        return (
            pltpu.make_async_copy(wg.at[:, cols], wguv.at[c, :, pl.ds(0, f)], w_sem.at[0, c]),
            pltpu.make_async_copy(wu.at[:, cols], wguv.at[c, :, pl.ds(f, f)], w_sem.at[1, c]),
            pltpu.make_async_copy(wd.at[cols, :], wdv.at[c], w_sem.at[2, c]),
        )

    @pl.loop(0, min(EARLY, chunks))
    def _(c):
        for copy in w_copies(c):
            copy.start()

    barrier = pltpu.get_barrier_semaphore()

    @pl.when(s > 0)
    def _():
        pl.semaphore_signal(barrier, inc=1, device_id={"shard": s - 1}, device_id_type=MESH)

    @pl.when(s < n - 1)
    def _():
        pl.semaphore_signal(barrier, inc=1, device_id={"shard": s + 1}, device_id_type=MESH)

    for k in range(1, n_dp):
        pl.semaphore_signal(
            barrier, inc=1, device_id={"dp": lax.rem(d + k, n_dp)}, device_id_type=MESH
        )

    chosen = routes[...] == e
    picked = jnp.max(chosen.astype(F32), axis=0, keepdims=True)
    weight_row = jnp.sum(jnp.where(chosen, prob[...], 0.0), axis=0, keepdims=True)
    weight = jnp.broadcast_to(weight_row, (t, t)).T[:, 0:1]
    rows_i = lax.broadcasted_iota(jnp.int32, (t, t), 0)
    cols_i = lax.broadcasted_iota(jnp.int32, (t, t), 1)
    above = (rows_i < cols_i).astype(F32).astype(BF16)
    rank = dot_nn(jnp.broadcast_to(picked, (CAP, t)).astype(BF16), above)
    slot = lax.broadcasted_iota(jnp.int32, (CAP, t), 0).astype(F32)
    dispatch = jnp.where(rank == slot, jnp.broadcast_to(picked, (CAP, t)), 0.0).astype(BF16)
    disp[...] = dispatch
    wgt[...] = jnp.broadcast_to(weight, wgt.shape)
    mine = pl.ds(pl.multiple_of(d * CAP, CAP), CAP)
    x_v[mine, :] = dot_nn(dispatch, tok[...]).astype(BF16)
    dz_tok = (weight * cot[...].astype(F32)).astype(BF16)
    dz_v[mine, :] = dot_nn(dispatch, dz_tok).astype(BF16)

    pl.semaphore_wait(barrier, (s > 0).astype(jnp.int32) + (s < n - 1).astype(jnp.int32) + (n_dp - 1))

    def slot_copy(ref, k, row, sem_row, to):
        rows = pl.ds(pl.multiple_of(row * CAP, CAP), CAP)
        return pltpu.make_async_remote_copy(
            src_ref=ref.at[rows], dst_ref=ref.at[rows],
            send_sem=xs_sem.at[k, to], recv_sem=xr_sem.at[k, sem_row],
            device_id={"dp": to}, device_id_type=MESH,
        )

    for j in range(1, n_dp):
        to = lax.rem(d + j, n_dp)
        slot_copy(x_v, 0, d, d, to).start()
        slot_copy(dz_v, 1, d, d, to).start()
    acc_o[...] = jnp.zeros_like(acc_o)
    acc_g[...] = jnp.zeros_like(acc_g)
    for j in range(1, n_dp):
        other = lax.rem(d + j, n_dp)
        slot_copy(x_v, 0, other, other, other).wait_recv()
        slot_copy(dz_v, 1, other, other, other).wait_recv()
    for j in range(1, n_dp):
        to = lax.rem(d + j, n_dp)
        slot_copy(x_v, 0, d, d, to).wait_send()
        slot_copy(dz_v, 1, d, d, to).wait_send()
    x_store = pltpu.make_async_copy(x_v, x_out, xo_sem.at[0])
    dz_store = pltpu.make_async_copy(dz_v, dz_out, xo_sem.at[1])
    x_store.start()
    dz_store.start()

    def rows_of(h):
        return pl.ds(h * half, half)

    def right_copy(c, h):
        here = lax.rem(c, n_stage)
        return pltpu.make_async_remote_copy(
            src_ref=to_right.at[here, rows_of(h)], dst_ref=from_left.at[c, rows_of(h)],
            send_sem=sr_sem.at[here, h], recv_sem=rr_sem.at[c, h],
            device_id={"shard": lax.min(s + 1, n - 1)}, device_id_type=MESH,
        )

    def left_copy(c, h):
        here = lax.rem(c, n_stage)
        return pltpu.make_async_remote_copy(
            src_ref=to_left.at[here, rows_of(h)], dst_ref=from_right.at[c, rows_of(h)],
            send_sem=sl_sem.at[here, h], recv_sem=rl_sem.at[c, h],
            device_id={"shard": lax.max(s - 1, 0)}, device_id_type=MESH,
        )

    def send(copy_of, buffer, c, h, value):
        @pl.when(c >= n_stage)
        def _():
            copy_of(c - n_stage, h).wait_send()

        buffer[lax.rem(c, n_stage), rows_of(h)] = value.astype(BF16)
        copy_of(c, h).start()

    @pl.loop(0, chunks + HOP * (n - 1))
    def _(i):
        @pl.when(i < chunks)
        def _():
            for copy in w_copies(i):
                copy.wait()

            @pl.when(i + EARLY < chunks)
            def _():
                for copy in w_copies(i + EARLY):
                    copy.start()

            p = lax.rem(i, n_part)
            part[p, :, 0:2 * f] = dot_nn(x_v[...], wguv[i])
            part[p, :, 2 * f:3 * f] = dot_nt(dz_v[...], wdv[i])

            @pl.when((s == 0) & (n > 1))
            def _():
                for h in range(HALVES):
                    send(right_copy, to_right, i, h, part[p, rows_of(h)])

            @pl.when((s == n - 1) & (n > 1))
            def _():
                for h in range(HALVES):
                    send(left_copy, to_left, i, h, part[p, rows_of(h)])

        r = i - HOP * s

        @pl.when((s > 0) & (r >= 0) & (r < chunks))
        def _():
            for h in range(HALVES):
                right_copy(r, h).wait_recv()

                @pl.when(s < n - 1)
                def _(h=h):
                    own = part[lax.rem(r, n_part), rows_of(h)]
                    send(right_copy, to_right, r, h, own + from_left[r, rows_of(h)].astype(F32))

        q = i - HOP * (n - 1 - s)

        @pl.when((s < n - 1) & (q >= 0) & (q < chunks))
        def _():
            for h in range(HALVES):
                left_copy(q, h).wait_recv()

                @pl.when(s > 0)
                def _(h=h):
                    own = part[lax.rem(q, n_part), rows_of(h)]
                    send(left_copy, to_left, q, h, own + from_right[q, rows_of(h)].astype(F32))

        c = i - HOP * lax.max(s, n - 1 - s)

        @pl.when((c >= 0) & (c < chunks))
        def _():
            p = lax.rem(c, n_part)

            @pl.when(s > 0)
            def _():
                part[p] += from_left[c].astype(F32)

            @pl.when(s < n - 1)
            def _():
                part[p] += from_right[c].astype(F32)

            gate = part[p, :, 0:f]
            up = part[p, :, f:2 * f]
            d_hidden = part[p, :, 2 * f:3 * f]
            sigma = jax.nn.sigmoid(gate)
            active = gate * sigma
            slope = sigma * (1.0 + gate * (1.0 - sigma))
            hidden = (active * up).astype(BF16)
            d_gate = (d_hidden * up * slope).astype(BF16)
            d_up = (d_hidden * active).astype(BF16)
            act[c, :, 0:f] = hidden
            act[c, :, f:2 * f] = d_gate
            act[c, :, 2 * f:3 * f] = d_up
            pltpu.make_async_copy(act.at[c], act_out.at[c], act_sem.at[c]).start()
            acc_o[...] += dot_nn(hidden, wdv[c])
            acc_g[...] += dot_nt(jnp.concatenate([d_gate, d_up], axis=1), wguv[c])

    stage[0] = acc_o[...].astype(BF16)
    stage[1] = acc_g[...].astype(BF16)

    def sum_copy(k, to, sender):
        return pltpu.make_async_remote_copy(
            src_ref=stage.at[k, pl.ds(pl.multiple_of(to * CAP, CAP), CAP)],
            dst_ref=landed.at[k, pl.ds(pl.multiple_of(sender * CAP, CAP), CAP)],
            send_sem=os_sem.at[k, to], recv_sem=or_sem.at[k, sender],
            device_id={"dp": to}, device_id_type=MESH,
        )

    for k in range(2):
        for j in range(1, n_dp):
            sum_copy(k, lax.rem(d + j, n_dp), d).start()
    for k in range(2):
        own = (acc_o, acc_g)[k][mine, :]
        for j in range(1, n_dp):
            other = lax.rem(d + j, n_dp)
            sum_copy(k, other, other).wait_recv()
            own = own + landed[k, pl.ds(pl.multiple_of(other * CAP, CAP), CAP), :].astype(F32)
        rows = dot_tn(disp[...], own.astype(BF16))
        if k == 0:
            rows = rows * wgt[:, 0:1]
        (mix_out, grad_out)[k][...] = rows.astype(BF16)

    for k in range(2):
        for j in range(1, n_dp):
            sum_copy(k, lax.rem(d + j, n_dp), d).wait_send()
    x_store.wait()
    dz_store.wait()

    @pl.loop(0, chunks)
    def _(c):
        pltpu.make_async_copy(act.at[c], act_out.at[c], act_sem.at[c]).wait()

    @pl.loop(max(chunks - n_stage, 0), chunks)
    def _(c):
        @pl.when(s < n - 1)
        def _():
            for h in range(HALVES):
                right_copy(c, h).wait_send()

        @pl.when(s > 0)
        def _():
            for h in range(HALVES):
                left_copy(c, h).wait_send()


def side_by_side(block):
    return jnp.concatenate([block[c] for c in range(block.shape[0])], axis=1)


def grads_in_kernel(d_gate, d_up, x, gate_out, up_out, x_t):
    @pl.when(pl.program_id(0) == 0)
    def _():
        x_t[...] = x[...].T

    gate_out[...] = dot_nn(x_t[...], side_by_side(d_gate))
    up_out[...] = dot_nn(x_t[...], side_by_side(d_up))


def grad_down_kernel(hidden, dz, down_out):
    down_out[...] = dot_tn(side_by_side(hidden), dz[...])


def expert_sum(value, n_expert, bits):
    for bit in bits:
        other = lax.ppermute(value, "expert", [(i, i ^ bit) for i in range(n_expert)])
        value = (value.astype(F32) + other.astype(F32)).astype(BF16)
    return value


def per_device(n, n_dp, n_expert, tokens, cotangent, routes, gate_prob, w_gate, w_up, w_down):
    t, dl = tokens.shape
    ffl = w_gate.shape[2]
    f = WIDTH
    chunks = ffl // f
    rows = n_dp * CAP
    n_part = min(HOP * (n - 1) + 1, chunks)
    n_stage = max(1, min(4, chunks // 2))
    vmem = pl.BlockSpec(memory_space=pltpu.VMEM)
    hbm = pl.BlockSpec(memory_space=pl.ANY)
    mix_part, grad_part, act, x_all, dz_all = pl.pallas_call(
        functools.partial(exchange_kernel, n, n_dp, chunks),
        out_shape=(
            jax.ShapeDtypeStruct((t, dl), BF16),
            jax.ShapeDtypeStruct((t, dl), BF16),
            jax.ShapeDtypeStruct((chunks, rows, 3 * f), BF16),
            jax.ShapeDtypeStruct((rows, dl), BF16),
            jax.ShapeDtypeStruct((rows, dl), BF16),
        ),
        in_specs=[vmem] * 4 + [hbm] * 3,
        out_specs=(vmem, vmem, hbm, hbm, hbm),
        scratch_shapes=[
            pltpu.VMEM((chunks, dl, 2 * f), BF16),
            pltpu.VMEM((chunks, f, dl), BF16),
            pltpu.VMEM((n_part, rows, 3 * f), F32),
            pltpu.VMEM((chunks, rows, 3 * f), BF16),
            pltpu.VMEM((chunks, rows, 3 * f), BF16),
            pltpu.VMEM((n_stage, rows, 3 * f), BF16),
            pltpu.VMEM((n_stage, rows, 3 * f), BF16),
            pltpu.VMEM((rows, dl), BF16),
            pltpu.VMEM((rows, dl), BF16),
            pltpu.VMEM((rows, dl), F32),
            pltpu.VMEM((rows, dl), F32),
            pltpu.VMEM((2, rows, dl), BF16),
            pltpu.VMEM((2, rows, dl), BF16),
            pltpu.VMEM((CAP, t), BF16),
            pltpu.VMEM((t, 128), F32),
            pltpu.SemaphoreType.DMA((3, chunks)),
            pltpu.SemaphoreType.DMA((n_stage, HALVES)),
            pltpu.SemaphoreType.DMA((chunks, HALVES)),
            pltpu.SemaphoreType.DMA((n_stage, HALVES)),
            pltpu.SemaphoreType.DMA((chunks, HALVES)),
            pltpu.SemaphoreType.DMA((chunks,)),
            pltpu.SemaphoreType.DMA((2,)),
            pltpu.SemaphoreType.DMA((2, n_dp)),
            pltpu.SemaphoreType.DMA((2, n_dp)),
            pltpu.SemaphoreType.DMA((2, n_dp)),
            pltpu.SemaphoreType.DMA((2, n_dp)),
        ],
        compiler_params=pltpu.CompilerParams(
            collective_id=0, has_side_effects=True, vmem_limit_bytes=63 * 1024 * 1024
        ),
        cost_estimate=pl.CostEstimate(
            flops=12 * rows * dl * ffl, bytes_accessed=6 * dl * ffl, transcendentals=rows * ffl
        ),
    )(tokens, cotangent, routes.T, gate_prob.T, w_gate[0], w_up[0], w_down[0])
    bits = [1 << k for k in range((n_expert - 1).bit_length())]
    mixed = expert_sum(mix_part, n_expert, bits)
    grad_tokens = expert_sum(grad_part, n_expert, bits[::-1])
    group = next(g for g in (4, 2, 1) if chunks % g == 0)
    full = pl.BlockSpec((rows, dl), lambda j: (0, 0))
    hidden_block, d_gate_block, d_up_block = (
        pl.BlockSpec((group, rows, f), lambda j, k=k: (j, 0, k)) for k in range(3)
    )
    wide = pl.BlockSpec((dl, group * f), lambda j: (0, j))
    roomy = pltpu.CompilerParams(vmem_limit_bytes=60 * 1024 * 1024)
    grad_gate, grad_up = pl.pallas_call(
        grads_in_kernel,
        grid=(chunks // group,),
        out_shape=(jax.ShapeDtypeStruct((dl, ffl), F32),) * 2,
        in_specs=[d_gate_block, d_up_block, full],
        out_specs=(wide, wide),
        scratch_shapes=[pltpu.VMEM((dl, rows), BF16)],
        compiler_params=roomy,
        cost_estimate=pl.CostEstimate(
            flops=4 * rows * dl * ffl, bytes_accessed=8 * dl * ffl, transcendentals=0
        ),
    )(act, act, x_all)
    grad_down = pl.pallas_call(
        grad_down_kernel,
        grid=(chunks // group,),
        out_shape=jax.ShapeDtypeStruct((ffl, dl), F32),
        in_specs=[hidden_block, full],
        out_specs=pl.BlockSpec((group * f, dl), lambda j: (j, 0)),
        compiler_params=roomy,
        cost_estimate=pl.CostEstimate(
            flops=2 * rows * dl * ffl, bytes_accessed=4 * dl * ffl, transcendentals=0
        ),
    )(act, dz_all)
    return (mixed, grad_tokens, grad_gate[None], grad_up[None], grad_down[None])


def solution(mesh):
    return jax.shard_map(
        functools.partial(per_device, mesh.shape["shard"], mesh.shape["dp"], mesh.shape["expert"]),
        mesh=mesh,
        in_specs=(
            P("dp", "shard"),
            P("dp", "shard"),
            P("dp", None),
            P("dp", None),
            P("expert", "shard", "dp"),
            P("expert", "shard", "dp"),
            P("expert", "dp", "shard"),
        ),
        out_specs=(
            P("dp", "shard"),
            P("dp", "shard"),
            P("expert", "shard", "dp"),
            P("expert", "shard", "dp"),
            P("expert", "dp", "shard"),
        ),
        check_vma=False,
    )
```

```python
import functools

import jax
import jax.numpy as jnp
from jax import lax
from jax.experimental import pallas as pl
from jax.experimental.pallas import tpu as pltpu
from jax.sharding import PartitionSpec as P

CAP = 96
WIDTH = 128
HOP = 4
EARLY = 8
HALVES = 2
MESH = pl.DeviceIdType.MESH
F32 = jnp.float32
BF16 = jnp.bfloat16


def dot_nn(left, right):
    return lax.dot_general(left, right, (((1,), (0,)), ((), ())), preferred_element_type=F32)


def dot_nt(left, right):
    return lax.dot_general(left, right, (((1,), (1,)), ((), ())), preferred_element_type=F32)


def dot_tn(left, right):
    return lax.dot_general(left, right, (((0,), (0,)), ((), ())), preferred_element_type=F32)


def exchange_kernel(
    n, n_dp, chunks,
    tok, cot, routes, prob, wg, wu, wd,
    mix_out, grad_out, act_out, x_out, dz_out,
    wguv, wdv, part, from_left, from_right, to_right, to_left,
    x_v, dz_v, acc_o, acc_g, stage, landed, disp, wgt,
    w_sem, sr_sem, rr_sem, sl_sem, rl_sem, act_sem, xo_sem,
    xs_sem, xr_sem, os_sem, or_sem,
):
    f = WIDTH
    s = lax.axis_index("shard")
    d = lax.axis_index("dp")
    e = lax.axis_index("expert")
    act = from_left
    n_part = part.shape[0]
    n_stage = to_right.shape[0]
    t = tok.shape[0]
    half = part.shape[1] // HALVES

    def w_copies(c):
        cols = pl.ds(pl.multiple_of(c * f, f), f)
        return (
            pltpu.make_async_copy(wg.at[:, cols], wguv.at[c, :, pl.ds(0, f)], w_sem.at[0, c]),
            pltpu.make_async_copy(wu.at[:, cols], wguv.at[c, :, pl.ds(f, f)], w_sem.at[1, c]),
            pltpu.make_async_copy(wd.at[cols, :], wdv.at[c], w_sem.at[2, c]),
        )

    @pl.loop(0, min(EARLY, chunks))
    def _(c):
        for copy in w_copies(c):
            copy.start()

    barrier = pltpu.get_barrier_semaphore()

    @pl.when(s > 0)
    def _():
        pl.semaphore_signal(barrier, inc=1, device_id={"shard": s - 1}, device_id_type=MESH)

    @pl.when(s < n - 1)
    def _():
        pl.semaphore_signal(barrier, inc=1, device_id={"shard": s + 1}, device_id_type=MESH)

    for k in range(1, n_dp):
        pl.semaphore_signal(
            barrier, inc=1, device_id={"dp": lax.rem(d + k, n_dp)}, device_id_type=MESH
        )

    chosen = routes[...] == e
    picked = jnp.max(chosen.astype(F32), axis=0, keepdims=True)
    weight_row = jnp.sum(jnp.where(chosen, prob[...], 0.0), axis=0, keepdims=True)
    weight = jnp.broadcast_to(weight_row, (t, t)).T[:, 0:1]
    rows_i = lax.broadcasted_iota(jnp.int32, (t, t), 0)
    cols_i = lax.broadcasted_iota(jnp.int32, (t, t), 1)
    above = (rows_i < cols_i).astype(F32).astype(BF16)
    rank = dot_nn(jnp.broadcast_to(picked, (CAP, t)).astype(BF16), above)
    slot = lax.broadcasted_iota(jnp.int32, (CAP, t), 0).astype(F32)
    dispatch = jnp.where(rank == slot, jnp.broadcast_to(picked, (CAP, t)), 0.0).astype(BF16)
    disp[...] = dispatch
    wgt[...] = jnp.broadcast_to(weight, wgt.shape)
    mine = pl.ds(pl.multiple_of(d * CAP, CAP), CAP)
    x_v[mine, :] = dot_nn(dispatch, tok[...]).astype(BF16)
    dz_tok = (weight * cot[...].astype(F32)).astype(BF16)
    dz_v[mine, :] = dot_nn(dispatch, dz_tok).astype(BF16)

    pl.semaphore_wait(barrier, (s > 0).astype(jnp.int32) + (s < n - 1).astype(jnp.int32) + (n_dp - 1))

    def slot_copy(ref, k, row, sem_row, to):
        rows = pl.ds(pl.multiple_of(row * CAP, CAP), CAP)
        return pltpu.make_async_remote_copy(
            src_ref=ref.at[rows], dst_ref=ref.at[rows],
            send_sem=xs_sem.at[k, to], recv_sem=xr_sem.at[k, sem_row],
            device_id={"dp": to}, device_id_type=MESH,
        )

    for j in range(1, n_dp):
        to = lax.rem(d + j, n_dp)
        slot_copy(x_v, 0, d, d, to).start()
        slot_copy(dz_v, 1, d, d, to).start()
    acc_o[...] = jnp.zeros_like(acc_o)
    acc_g[...] = jnp.zeros_like(acc_g)
    for j in range(1, n_dp):
        other = lax.rem(d + j, n_dp)
        slot_copy(x_v, 0, other, other, other).wait_recv()
        slot_copy(dz_v, 1, other, other, other).wait_recv()
    for j in range(1, n_dp):
        to = lax.rem(d + j, n_dp)
        slot_copy(x_v, 0, d, d, to).wait_send()
        slot_copy(dz_v, 1, d, d, to).wait_send()
    x_store = pltpu.make_async_copy(x_v, x_out, xo_sem.at[0])
    dz_store = pltpu.make_async_copy(dz_v, dz_out, xo_sem.at[1])
    x_store.start()
    dz_store.start()

    def rows_of(h):
        return pl.ds(h * half, half)

    def right_copy(c, h):
        here = lax.rem(c, n_stage)
        return pltpu.make_async_remote_copy(
            src_ref=to_right.at[here, rows_of(h)], dst_ref=from_left.at[c, rows_of(h)],
            send_sem=sr_sem.at[here, h], recv_sem=rr_sem.at[c, h],
            device_id={"shard": lax.min(s + 1, n - 1)}, device_id_type=MESH,
        )

    def left_copy(c, h):
        here = lax.rem(c, n_stage)
        return pltpu.make_async_remote_copy(
            src_ref=to_left.at[here, rows_of(h)], dst_ref=from_right.at[c, rows_of(h)],
            send_sem=sl_sem.at[here, h], recv_sem=rl_sem.at[c, h],
            device_id={"shard": lax.max(s - 1, 0)}, device_id_type=MESH,
        )

    def send(copy_of, buffer, c, h, value):
        @pl.when(c >= n_stage)
        def _():
            copy_of(c - n_stage, h).wait_send()

        buffer[lax.rem(c, n_stage), rows_of(h)] = value.astype(BF16)
        copy_of(c, h).start()

    @pl.loop(0, chunks + HOP * (n - 1))
    def _(i):
        @pl.when(i < chunks)
        def _():
            for copy in w_copies(i):
                copy.wait()

            @pl.when(i + EARLY < chunks)
            def _():
                for copy in w_copies(i + EARLY):
                    copy.start()

            p = lax.rem(i, n_part)
            part[p, :, 0:2 * f] = dot_nn(x_v[...], wguv[i])
            part[p, :, 2 * f:3 * f] = dot_nt(dz_v[...], wdv[i])

            @pl.when((s == 0) & (n > 1))
            def _():
                for h in range(HALVES):
                    send(right_copy, to_right, i, h, part[p, rows_of(h)])

            @pl.when((s == n - 1) & (n > 1))
            def _():
                for h in range(HALVES):
                    send(left_copy, to_left, i, h, part[p, rows_of(h)])

        r = i - HOP * s

        @pl.when((s > 0) & (r >= 0) & (r < chunks))
        def _():
            for h in range(HALVES):
                right_copy(r, h).wait_recv()

                @pl.when(s < n - 1)
                def _(h=h):
                    own = part[lax.rem(r, n_part), rows_of(h)]
                    send(right_copy, to_right, r, h, own + from_left[r, rows_of(h)].astype(F32))

        q = i - HOP * (n - 1 - s)

        @pl.when((s < n - 1) & (q >= 0) & (q < chunks))
        def _():
            for h in range(HALVES):
                left_copy(q, h).wait_recv()

                @pl.when(s > 0)
                def _(h=h):
                    own = part[lax.rem(q, n_part), rows_of(h)]
                    send(left_copy, to_left, q, h, own + from_right[q, rows_of(h)].astype(F32))

        c = i - HOP * lax.max(s, n - 1 - s)

        @pl.when((c >= 0) & (c < chunks))
        def _():
            p = lax.rem(c, n_part)

            @pl.when(s > 0)
            def _():
                part[p] += from_left[c].astype(F32)

            @pl.when(s < n - 1)
            def _():
                part[p] += from_right[c].astype(F32)

            gate = part[p, :, 0:f]
            up = part[p, :, f:2 * f]
            d_hidden = part[p, :, 2 * f:3 * f]
            sigma = jax.nn.sigmoid(gate)
            active = gate * sigma
            slope = sigma * (1.0 + gate * (1.0 - sigma))
            hidden = (active * up).astype(BF16)
            d_gate = (d_hidden * up * slope).astype(BF16)
            d_up = (d_hidden * active).astype(BF16)
            act[c, :, 0:f] = hidden
            act[c, :, f:2 * f] = d_gate
            act[c, :, 2 * f:3 * f] = d_up
            pltpu.make_async_copy(act.at[c], act_out.at[c], act_sem.at[c]).start()
            acc_o[...] += dot_nn(hidden, wdv[c])
            acc_g[...] += dot_nt(jnp.concatenate([d_gate, d_up], axis=1), wguv[c])

    stage[0] = acc_o[...].astype(BF16)
    stage[1] = acc_g[...].astype(BF16)

    def sum_copy(k, to, sender):
        return pltpu.make_async_remote_copy(
            src_ref=stage.at[k, pl.ds(pl.multiple_of(to * CAP, CAP), CAP)],
            dst_ref=landed.at[k, pl.ds(pl.multiple_of(sender * CAP, CAP), CAP)],
            send_sem=os_sem.at[k, to], recv_sem=or_sem.at[k, sender],
            device_id={"dp": to}, device_id_type=MESH,
        )

    for k in range(2):
        for j in range(1, n_dp):
            sum_copy(k, lax.rem(d + j, n_dp), d).start()
    for k in range(2):
        own = (acc_o, acc_g)[k][mine, :]
        for j in range(1, n_dp):
            other = lax.rem(d + j, n_dp)
            sum_copy(k, other, other).wait_recv()
            own = own + landed[k, pl.ds(pl.multiple_of(other * CAP, CAP), CAP), :].astype(F32)
        rows = dot_tn(disp[...], own.astype(BF16))
        if k == 0:
            rows = rows * wgt[:, 0:1]
        (mix_out, grad_out)[k][...] = rows.astype(BF16)

    for k in range(2):
        for j in range(1, n_dp):
            sum_copy(k, lax.rem(d + j, n_dp), d).wait_send()
    x_store.wait()
    dz_store.wait()

    @pl.loop(0, chunks)
    def _(c):
        pltpu.make_async_copy(act.at[c], act_out.at[c], act_sem.at[c]).wait()

    @pl.loop(max(chunks - n_stage, 0), chunks)
    def _(c):
        @pl.when(s < n - 1)
        def _():
            for h in range(HALVES):
                right_copy(c, h).wait_send()

        @pl.when(s > 0)
        def _():
            for h in range(HALVES):
                left_copy(c, h).wait_send()


def side_by_side(block):
    return jnp.concatenate([block[c] for c in range(block.shape[0])], axis=1)


def grads_in_kernel(d_gate, d_up, x, gate_out, up_out, x_t):
    @pl.when(pl.program_id(0) == 0)
    def _():
        x_t[...] = x[...].T

    gate_out[...] = dot_nn(x_t[...], side_by_side(d_gate))
    up_out[...] = dot_nn(x_t[...], side_by_side(d_up))


def grad_down_kernel(hidden, dz, down_out):
    down_out[...] = dot_tn(side_by_side(hidden), dz[...])


def expert_sum(value, n_expert, bits):
    for bit in bits:
        other = lax.ppermute(value, "expert", [(i, i ^ bit) for i in range(n_expert)])
        value = (value.astype(F32) + other.astype(F32)).astype(BF16)
    return value


def per_device(n, n_dp, n_expert, tokens, cotangent, routes, gate_prob, w_gate, w_up, w_down):
    t, dl = tokens.shape
    ffl = w_gate.shape[2]
    f = WIDTH
    chunks = ffl // f
    rows = n_dp * CAP
    n_part = min(HOP * (n - 1) + 1, chunks)
    n_stage = max(1, min(8, chunks // 2))
    vmem = pl.BlockSpec(memory_space=pltpu.VMEM)
    hbm = pl.BlockSpec(memory_space=pl.ANY)
    mix_part, grad_part, act, x_all, dz_all = pl.pallas_call(
        functools.partial(exchange_kernel, n, n_dp, chunks),
        out_shape=(
            jax.ShapeDtypeStruct((t, dl), BF16),
            jax.ShapeDtypeStruct((t, dl), BF16),
            jax.ShapeDtypeStruct((chunks, rows, 3 * f), BF16),
            jax.ShapeDtypeStruct((rows, dl), BF16),
            jax.ShapeDtypeStruct((rows, dl), BF16),
        ),
        in_specs=[vmem] * 4 + [hbm] * 3,
        out_specs=(vmem, vmem, hbm, hbm, hbm),
        scratch_shapes=[
            pltpu.VMEM((chunks, dl, 2 * f), BF16),
            pltpu.VMEM((chunks, f, dl), BF16),
            pltpu.VMEM((n_part, rows, 3 * f), F32),
            pltpu.VMEM((chunks, rows, 3 * f), BF16),
            pltpu.VMEM((chunks, rows, 3 * f), BF16),
            pltpu.VMEM((n_stage, rows, 3 * f), BF16),
            pltpu.VMEM((n_stage, rows, 3 * f), BF16),
            pltpu.VMEM((rows, dl), BF16),
            pltpu.VMEM((rows, dl), BF16),
            pltpu.VMEM((rows, dl), F32),
            pltpu.VMEM((rows, dl), F32),
            pltpu.VMEM((2, rows, dl), BF16),
            pltpu.VMEM((2, rows, dl), BF16),
            pltpu.VMEM((CAP, t), BF16),
            pltpu.VMEM((t, 128), F32),
            pltpu.SemaphoreType.DMA((3, chunks)),
            pltpu.SemaphoreType.DMA((n_stage, HALVES)),
            pltpu.SemaphoreType.DMA((chunks, HALVES)),
            pltpu.SemaphoreType.DMA((n_stage, HALVES)),
            pltpu.SemaphoreType.DMA((chunks, HALVES)),
            pltpu.SemaphoreType.DMA((chunks,)),
            pltpu.SemaphoreType.DMA((2,)),
            pltpu.SemaphoreType.DMA((2, n_dp)),
            pltpu.SemaphoreType.DMA((2, n_dp)),
            pltpu.SemaphoreType.DMA((2, n_dp)),
            pltpu.SemaphoreType.DMA((2, n_dp)),
        ],
        compiler_params=pltpu.CompilerParams(
            collective_id=0, has_side_effects=True, vmem_limit_bytes=63 * 1024 * 1024
        ),
        cost_estimate=pl.CostEstimate(
            flops=12 * rows * dl * ffl, bytes_accessed=6 * dl * ffl, transcendentals=rows * ffl
        ),
    )(tokens, cotangent, routes.T, gate_prob.T, w_gate[0], w_up[0], w_down[0])
    bits = [1 << k for k in range((n_expert - 1).bit_length())]
    mixed = expert_sum(mix_part, n_expert, bits)
    grad_tokens = expert_sum(grad_part, n_expert, bits[::-1])
    group = next(g for g in (4, 2, 1) if chunks % g == 0)
    full = pl.BlockSpec((rows, dl), lambda j: (0, 0))
    hidden_block, d_gate_block, d_up_block = (
        pl.BlockSpec((group, rows, f), lambda j, k=k: (j, 0, k)) for k in range(3)
    )
    wide = pl.BlockSpec((dl, group * f), lambda j: (0, j))
    roomy = pltpu.CompilerParams(vmem_limit_bytes=60 * 1024 * 1024)
    grad_gate, grad_up = pl.pallas_call(
        grads_in_kernel,
        grid=(chunks // group,),
        out_shape=(jax.ShapeDtypeStruct((dl, ffl), F32),) * 2,
        in_specs=[d_gate_block, d_up_block, full],
        out_specs=(wide, wide),
        scratch_shapes=[pltpu.VMEM((dl, rows), BF16)],
        compiler_params=roomy,
        cost_estimate=pl.CostEstimate(
            flops=4 * rows * dl * ffl, bytes_accessed=8 * dl * ffl, transcendentals=0
        ),
    )(act, act, x_all)
    grad_down = pl.pallas_call(
        grad_down_kernel,
        grid=(chunks // group,),
        out_shape=jax.ShapeDtypeStruct((ffl, dl), F32),
        in_specs=[hidden_block, full],
        out_specs=pl.BlockSpec((group * f, dl), lambda j: (j, 0)),
        compiler_params=roomy,
        cost_estimate=pl.CostEstimate(
            flops=2 * rows * dl * ffl, bytes_accessed=4 * dl * ffl, transcendentals=0
        ),
    )(act, dz_all)
    return (mixed, grad_tokens, grad_gate[None], grad_up[None], grad_down[None])


def solution(mesh):
    return jax.shard_map(
        functools.partial(per_device, mesh.shape["shard"], mesh.shape["dp"], mesh.shape["expert"]),
        mesh=mesh,
        in_specs=(
            P("dp", "shard"),
            P("dp", "shard"),
            P("dp", None),
            P("dp", None),
            P("expert", "shard", "dp"),
            P("expert", "shard", "dp"),
            P("expert", "dp", "shard"),
        ),
        out_specs=(
            P("dp", "shard"),
            P("dp", "shard"),
            P("expert", "shard", "dp"),
            P("expert", "shard", "dp"),
            P("expert", "dp", "shard"),
        ),
        check_vma=False,
    )
```
